128 devices in a mesh: group: 2 (over z_lo), dp: 8 (over z_hi, y), tensor: 8 (over x, core).
Axes of the slice: x: 4, y: 4, z: 4 (z_hi: 2, z_lo: 2; z = z_hi * 2 + z_lo), core: 2. Of those that a mesh axis runs over, the one named last changes fastest.
Arguments:
- context: bfloat16 [1536, 8192], P('dp', ('group', 'tensor')), may hold values from -6 to 6
- low: bfloat16 [1536, 8192], P(('group', 'tensor'), 'dp'), may hold values from -6 to 6
- mid: bfloat16 [1536, 8192], P(('group', 'tensor'), 'dp'), may hold values from -6 to 6
- top: bfloat16 [1536, 8192], P('dp', ('group', 'tensor')), may hold values from -18 to 18
- segments: int32 [1536], replicated, may hold values from 0 to 15, never falling along the last dimension, each value on 1 to 192 neighbouring positions
- output_weight: bfloat16 [8192, 8192], P(('group', 'tensor'), 'dp'), may hold values from -0.0625 to 0.0625
- join_weight: bfloat16 [3, 8192, 8192], P(None, 'dp', ('group', 'tensor')), may hold values from -0.0390625 to 0.0390625
- inner_weight: bfloat16 [8192, 14336], P(('group', 'tensor'), 'dp'), may hold values from -0.0625 to 0.0625
- outer_weight: bfloat16 [14336, 8192], P('dp', ('group', 'tensor')), may hold values from -0.046875 to 0.046875
- norm_gain: float32 [8192], P(('group', 'tensor')), may hold values from 0.25 to 1.75
Outputs:
- mean_error: float32 [], replicated
- grad_join: float32 [3, 8192, 8192], P(None, 'dp', ('group', 'tensor'))
- grad_inner: float32 [8192, 14336], P(('group', 'tensor'), 'dp')
- grad_outer: float32 [14336, 8192], P('dp', ('group', 'tensor'))
The draws below stay inside these ranges and needn't reach their ends.
Inputs may be any that keep to these rules, and one draw needn't show every extreme that they name: `segments`: segment numbers never fall along the tokens; each document spans 1 to 192 tokens.
All inputs are finite; a program needn't handle non-finite values.
Results may differ from the reference program's by a relative error of at most 0.034.
Values may be sent and summed in bfloat16 or wider, within the bound.
No kernel may reach another device: no remote copies, remote signals or barrier semaphores. Data moves between devices by JAX's collectives and lax.ppermute only.
A program may use at most 192 MiB of HBM per device.

```python
import math
import jax
import jax.numpy as jnp
import numpy as np
from jax import lax

D = 8192
FF = 14336
STEPS = 2
TOKENS = 1536
BLOCKS = 16


def draw_top(key, part):
    key = jax.random.fold_in(key, 11)
    column = jnp.arange(D, dtype=jnp.float32) / D
    values = jnp.clip(jax.random.normal(key, (TOKENS, D), jnp.float32), -6.0, 6.0)
    values = values * jnp.exp(column * jnp.log(3.0))[None, :]
    return values.astype(jnp.bfloat16)


def steps_of(own_key, shape, split, least, high):
    loudness, own = 1.0, jax.random.fold_in(own_key, 6)
    for dim, shards_of in split:
        steps = jnp.exp(jax.random.uniform(jax.random.fold_in(own, dim), (shards_of,), jnp.float32, least / len(split), high / len(split)))
        loudness = loudness * jnp.repeat(steps, shape[dim] // shards_of).reshape([-1 if axis == dim else 1 for axis in range(len(shape))])
    return loudness


def split_up(number_of, total, bound, slope):
    weights = [(1 << 20) // math.isqrt(standing ** slope) + 1 for standing in range(2, number_of + 1)]
    surplus, holding = total - bound - (number_of - 1), [1] * (number_of - 1)
    while surplus > 0:
        candidates = [i for i in range(number_of - 1) if holding[i] < bound]
        whole, remaining = sum([weights[i] for i in candidates]), surplus
        for i in candidates:
            extra = min(bound - holding[i], max(1, remaining * weights[i] // whole), surplus)
            holding[i] = holding[i] + extra
            surplus = surplus - extra
    return np.array([bound] + holding)


def uneven(rng, count, total, reach, skew):
    if count == 2:
        one = jax.random.randint(rng, (), max(1, total - reach), min(reach, total - 1) + 1)
        return jnp.stack([one, total - one])
    lengths = jnp.asarray(split_up(count, total, reach, skew), jnp.int32)
    twos = (count - 1) // 2
    giver, sink = lengths[1:1 + 2 * twos:2], lengths[2:2 + 2 * twos:2]
    room = jnp.minimum(giver - 1, reach - sink)
    passed = jax.random.randint(jax.random.fold_in(rng, 1), (twos,), 0, 1 << 20) % (room + 1)
    lengths = lengths.at[1:1 + 2 * twos:2].set(giver - passed).at[2:2 + 2 * twos:2].set(sink + passed)
    return lengths[jax.random.permutation(jax.random.fold_in(rng, 2), count)]


def gaussian(own_key, extent, scale, most, split=(), kind=jnp.bfloat16):
    result = scale * jax.random.normal(own_key, extent, jnp.float32)
    if split:
        result = result * steps_of(own_key, extent, split, -0.22, 0.18)
    return jnp.clip(result, -most, most).astype(kind)


def setup_inputs(seed: int = 0) -> dict:
    keys = jax.random.split(jax.random.key(seed), 11)
    context = gaussian(keys[0], (TOKENS, D), 1.0, 6.0, ((0, 8), (1, 16)))
    low = gaussian(keys[1], (TOKENS, D), 1.0, 6.0, ((0, 16), (1, 8)))
    mid = gaussian(keys[2], (TOKENS, D), 1.0, 6.0, ((0, 16), (1, 8)))
    top = draw_top(jax.random.fold_in(keys[10], 71), 0)
    segments = jnp.searchsorted(jnp.cumsum(uneven(keys[4], 16, TOKENS, TOKENS // 8, 1)), jnp.arange(TOKENS), side="right").astype(jnp.int32)
    output_weight = gaussian(keys[5], (D, D), D ** -0.5, 0.0625, ((0, 16), (1, 8)))
    join_weight = gaussian(keys[6], (3, D, D), (3 * D) ** -0.5, 0.0390625, ((1, 8), (2, 16)))
    inner_weight = gaussian(keys[7], (D, FF), D ** -0.5, 0.0625, ((0, 16), (1, 8)))
    outer_weight = gaussian(keys[8], (FF, D), FF ** -0.5, 0.046875, ((0, 8), (1, 16)))
    norm_gain = jnp.clip(1.0 + 0.15 * jax.random.normal(keys[9], (D,), jnp.float32), 0.25, 1.75)
    return dict(context=context, low=low, mid=mid, top=top, segments=segments, output_weight=output_weight, join_weight=join_weight, inner_weight=inner_weight, outer_weight=outer_weight, norm_gain=norm_gain)


epsilon = 1e-05

def block_sum(rows, weight):
    width = rows.shape[1] // BLOCKS
    row_parts = rows.reshape(rows.shape[0], BLOCKS, width).transpose(1, 0, 2)
    weight_parts = weight.reshape(BLOCKS, width, weight.shape[1])

    def add_block(total, operands):
        part = jnp.dot(operands[0], operands[1], preferred_element_type=jnp.float32)
        part = lax.optimization_barrier(part.astype(jnp.bfloat16))
        return (total + part.astype(jnp.float32), None)
    start = jnp.zeros((rows.shape[0], weight.shape[1]), jnp.float32)
    total, unused = lax.scan(add_block, start, (row_parts, weight_parts))
    return total

def reference(context, low, mid, top, segments, output_weight, join_weight, inner_weight, outer_weight, norm_gain):
    tokens = context.shape[0]
    high = (mid.astype(jnp.float32) + block_sum(context, output_weight)).astype(jnp.bfloat16)
    joined = jnp.dot(low, join_weight[0], preferred_element_type=jnp.float32)
    joined = joined + jnp.dot(mid, join_weight[1], preferred_element_type=jnp.float32)
    joined = joined + jnp.dot(high, join_weight[2], preferred_element_type=jnp.float32)
    state = joined.astype(jnp.bfloat16)
    seg_pad = jnp.concatenate([segments.astype(jnp.int32), jnp.full((STEPS + 1,), -1, jnp.int32)])
    top_pad = jnp.concatenate([top.astype(jnp.float32), jnp.zeros((STEPS + 1, D), jnp.float32)])
    saved = []
    total = jnp.zeros((), jnp.float32)
    for step in range(STEPS):
        xfull = state.astype(jnp.float32)
        mean_sq = lax.optimization_barrier(jnp.mean(xfull * xfull, axis=1, keepdims=True))
        scale = lax.rsqrt(mean_sq + epsilon)
        normed = (xfull * scale * norm_gain).astype(jnp.bfloat16)
        inner = block_sum(normed, inner_weight)
        active = jax.nn.silu(inner).astype(jnp.bfloat16)
        update = jnp.dot(active, outer_weight, preferred_element_type=jnp.float32)
        following = (xfull + update).astype(jnp.bfloat16)
        valid = (seg_pad[step + 1:step + 1 + tokens] == segments).astype(jnp.float32)
        error = valid[:, None] * (following.astype(jnp.float32) - top_pad[step + 1:step + 1 + tokens])
        total = total + jnp.sum(error * error)
        saved.append((xfull, scale, normed, inner, active, error))
        state = following
    mean_error = total / (STEPS * tokens * D)
    rate = 1.0 / tokens ** 0.5
    grad = jnp.zeros((tokens, D), jnp.float32)
    grad_inner = jnp.zeros((D, FF), jnp.float32)
    grad_outer = jnp.zeros((FF, D), jnp.float32)
    for step in reversed(range(STEPS)):
        xfull, scale, normed, inner, active, error = saved[step]
        grad = grad + rate * error
        grad_half = grad.astype(jnp.bfloat16)
        grad_outer = grad_outer + jnp.dot(active.T, grad_half, preferred_element_type=jnp.float32)
        back_act = block_sum(grad_half, outer_weight.T)
        sigma = jax.nn.sigmoid(inner)
        grad_in = (back_act * sigma * (1.0 + inner * (1.0 - sigma))).astype(jnp.bfloat16)
        grad_inner = grad_inner + jnp.dot(normed.T, grad_in, preferred_element_type=jnp.float32)
        back_norm = jnp.dot(grad_in, inner_weight.T, preferred_element_type=jnp.float32)
        product = lax.optimization_barrier(jnp.sum(back_norm * norm_gain * xfull, axis=1, keepdims=True))
        grad = grad + scale * norm_gain * back_norm - xfull * scale ** 3 * product / D
    grad_half = grad.astype(jnp.bfloat16)
    grad_join = jnp.stack([jnp.dot(source.T, grad_half, preferred_element_type=jnp.float32) for source in (low, mid, high)])
    return (mean_error, grad_join, grad_inner, grad_outer)
```

```python
import math

import jax
import jax.numpy as jnp
from jax import lax
from jax.sharding import PartitionSpec as P

D = 8192
STEPS = 2
epsilon = 1e-05

F32 = jnp.float32
BF16 = jnp.bfloat16
UNITS = ("group", "tensor")
EVERY = ("group", "dp", "tensor")


def chip_peers():
    n = lax.axis_size(UNITS)
    return [[chip * 2 + core for chip in range(n // 2)] for core in range(2)]


def other_core(values):
    n = lax.axis_size("tensor")
    return lax.ppermute(values, "tensor", [(i, i ^ 1) for i in range(n)])


def other_group(values):
    return lax.ppermute(values, "group", [(0, 1), (1, 0)])


def swap_axes(values):
    groups, n = lax.axis_size("group"), lax.axis_size("dp")
    route = [
        ((k * n + a) * n + b, (k * n + b) * n + a)
        for k in range(groups)
        for a in range(n)
        for b in range(n)
    ]
    return lax.ppermute(values, EVERY, route)


def shifted(block, axis, distance):
    devices = range(lax.axis_size(axis))
    route = [(i - distance, i) for i in devices if i - distance in devices]
    return lax.ppermute(block, axis, route)


def copies(values, axis, count, groups=None):
    sent = jnp.broadcast_to(values[None], (count,) + values.shape)
    return lax.all_to_all(sent, axis, 0, 0, tiled=True, axis_index_groups=groups)


def total_of(blocks, axis, groups=None):
    got = lax.all_to_all(blocks, axis, 0, 0, tiled=True, axis_index_groups=groups)
    return jnp.sum(got.astype(F32), axis=0)


def contract_rows(left, right):
    return lax.dot_general(left, right, (((0,), (0,)), ((), ())), preferred_element_type=F32)


def to_feature_owners(blocks):
    return lax.all_to_all(blocks, "tensor", 0, 0, tiled=True)


def row_gather(values, axis):
    block = lax.optimization_barrier(jnp.broadcast_to(values[None], (64, values.shape[0])))
    got = lax.optimization_barrier(lax.all_gather(block, axis, axis=0, tiled=True))
    return got.reshape((lax.axis_size(axis), 64, values.shape[0]))[:, :1]


def after(values, *earlier):
    for other in earlier:
        values = values + (0.0 * other.reshape(-1)[0].astype(F32)).astype(values.dtype)
    return values


def body(
    context,
    low,
    mid,
    top,
    segments,
    output_weight,
    join_weight,
    inner_weight,
    outer_weight,
    norm_gain,
):
    n_dp = lax.axis_size("dp")
    n_tensor = lax.axis_size("tensor")
    chips = lax.axis_size(UNITS) // 2
    rows, width = context.shape
    rows_b, width_b = low.shape
    tokens = rows * n_dp
    core = lax.axis_index("tensor") % 2
    peers = chip_peers()
    place = lax.axis_index("tensor") * rows

    own_top = swap_axes(top)
    gains = row_gather(norm_gain, "tensor")
    gain = lax.dynamic_index_in_dim(gains, lax.axis_index("dp"), 0, keepdims=False)
    following_top = shifted(own_top[: STEPS + 1], "tensor", -1)
    top_ext = jnp.concatenate([own_top, following_top], axis=0).astype(F32)
    seg_pad = jnp.concatenate([segments, jnp.full((STEPS + 1,), -1, jnp.int32)])
    seg_window = lax.dynamic_slice_in_dim(seg_pad, place, rows + STEPS + 1, 0)

    low_mid = lax.all_gather(jnp.stack([low, mid]), UNITS, axis=1, tiled=True)
    inner_all = lax.all_gather(inner_weight, "tensor", axis=0, tiled=True).reshape(
        n_tensor, width, -1
    )
    outer_all = lax.all_gather(outer_weight, "tensor", axis=0, tiled=False)

    context_all = copies(context, "dp", n_dp).reshape(tokens, width)
    part = jnp.dot(context_all, output_weight, preferred_element_type=F32).astype(BF16)
    part = part.reshape(chips, 2, rows_b, width_b)
    kept = lax.dynamic_index_in_dim(part, core, 1, keepdims=False)
    given = lax.dynamic_index_in_dim(part, 1 - core, 1, keepdims=False)
    part = (kept.astype(F32) + other_core(given).astype(F32)).astype(BF16)
    high = after(mid.astype(F32), following_top) + total_of(part, UNITS, peers)
    high = high.astype(BF16)
    high_own = copies(high, UNITS, chips, peers)
    high_other = other_core(high_own)
    high_all = jnp.where(
        core == 0,
        jnp.stack([high_own, high_other], axis=1),
        jnp.stack([high_other, high_own], axis=1),
    ).reshape(tokens, width_b)
    hidden_all = (low_mid[0], low_mid[1], high_all)

    joined = jnp.dot(hidden_all[0], join_weight[0], preferred_element_type=F32)
    joined = joined + jnp.dot(hidden_all[1], join_weight[1], preferred_element_type=F32)
    joined = joined + jnp.dot(hidden_all[2], join_weight[2], preferred_element_type=F32)
    joined = total_of(joined.astype(BF16).reshape(n_dp, rows, width), "dp")
    state = swap_axes(joined.astype(BF16))

    saved = []
    total = jnp.zeros((), F32)
    for step in range(STEPS):
        xfull = state.astype(F32)
        x_all = copies(state, "dp", n_dp).astype(F32)
        sums = jnp.sum(x_all * x_all, axis=(0, 2))
        sums = sums + other_group(sums)
        scale = lax.rsqrt(sums / D + epsilon)[:, None]
        normed = (x_all * scale * gains).astype(BF16)
        part = jnp.einsum("brf,bfu->ru", normed, inner_all, preferred_element_type=F32)
        inner = part + other_group(part.astype(BF16)).astype(F32)
        active = jax.nn.silu(inner).astype(BF16)
        update = jnp.einsum("ru,buf->brf", active, outer_all, preferred_element_type=F32)
        update = total_of(update.astype(BF16), "dp")
        following = (xfull + update).astype(BF16)
        valid = (seg_window[step + 1 : step + 1 + rows] == seg_window[:rows]).astype(F32)
        error = valid[:, None] * (following.astype(F32) - top_ext[step + 1 : step + 1 + rows])
        total = total + jnp.sum(error * error)
        active_all = lax.all_gather(active, "tensor", axis=0, tiled=True)
        saved.append((xfull, scale, normed, inner, active_all, error))
        state = following
    rate = 1.0 / math.sqrt(tokens)
    grad = jnp.zeros((rows, width), F32)
    grad_inner = jnp.zeros(inner_weight.shape, F32)
    grad_outer = jnp.zeros(outer_weight.shape, F32)
    for step in reversed(range(STEPS)):
        xfull, scale, normed, inner, active_all, error = saved[step]
        grad = grad + rate * error
        grad_all = copies(grad.astype(BF16), "dp", n_dp)
        part = jnp.einsum("brf,buf->ru", grad_all, outer_all, preferred_element_type=F32)
        back_act = part + other_group(part.astype(BF16)).astype(F32)
        sigma = jax.nn.sigmoid(inner)
        grad_in = (back_act * sigma * (1.0 + inner * (1.0 - sigma))).astype(BF16)
        moved = jnp.sum(grad_in.astype(F32) * inner, axis=1)
        moved = jnp.concatenate([moved, jnp.full((64,), total)]).reshape(2, 128)
        moved = jnp.sum(copies(moved, "dp", n_dp), axis=0).reshape(256)
        total_dp = moved[rows:]
        moved = moved[:rows, None]
        back = jnp.einsum("ru,bfu->brf", grad_in, inner_all, preferred_element_type=F32)
        back_norm = total_of(back.astype(BF16), "dp")
        grad = grad + scale * gain * back_norm - xfull * scale**2 * moved / D
        grad_in_all = lax.all_gather(grad_in, "tensor", axis=0, tiled=True)
        grad_tokens = to_feature_owners(grad_all).reshape(tokens, width)
        grad_outer = grad_outer + contract_rows(active_all, grad_tokens)
        normed_all = to_feature_owners(normed).reshape(tokens, width)
        grad_inner = grad_inner + contract_rows(normed_all, grad_in_all)
    for k in (1, 2, 4):
        total_dp = total_dp + lax.ppermute(
            total_dp, "tensor", [(i, i ^ k) for i in range(n_tensor)]
        )
    mean_error = (total_dp + other_group(total_dp))[0] / (STEPS * tokens * D)
    grad_tokens = copies(swap_axes(grad.astype(BF16)), "dp", n_dp).reshape(tokens, width)
    grad_join = jnp.stack([contract_rows(source, grad_tokens) for source in hidden_all])
    return (mean_error, grad_join, grad_inner, grad_outer)


def solution(mesh):
    in_specs = (
        P("dp", ("group", "tensor")),
        P(("group", "tensor"), "dp"),
        P(("group", "tensor"), "dp"),
        P("dp", ("group", "tensor")),
        P(),
        P(("group", "tensor"), "dp"),
        P(None, "dp", ("group", "tensor")),
        P(("group", "tensor"), "dp"),
        P("dp", ("group", "tensor")),
        P(("group", "tensor")),
    )
    out_specs = (
        P(),
        P(None, "dp", ("group", "tensor")),
        P(("group", "tensor"), "dp"),
        P("dp", ("group", "tensor")),
    )
    return jax.shard_map(body, mesh=mesh, in_specs=in_specs, out_specs=out_specs, check_vma=False)
```

```python
import functools
import math

import jax
import jax.numpy as jnp
from jax import lax
from jax.experimental import pallas as pl
from jax.experimental.pallas import tpu as pltpu
from jax.sharding import PartitionSpec as P

D = 8192
STEPS = 2
epsilon = 1e-05

F32 = jnp.float32
BF16 = jnp.bfloat16
UNITS = ("group", "tensor")
EVERY = ("group", "dp", "tensor")


def chip_peers():
    n = lax.axis_size(UNITS)
    return [[chip * 2 + core for chip in range(n // 2)] for core in range(2)]


def other_core(values):
    n = lax.axis_size("tensor")
    return lax.ppermute(values, "tensor", [(i, i ^ 1) for i in range(n)])


def other_group(values):
    return lax.ppermute(values, "group", [(0, 1), (1, 0)])


def swap_axes(values):
    groups, n = lax.axis_size("group"), lax.axis_size("dp")
    route = [
        ((k * n + a) * n + b, (k * n + b) * n + a)
        for k in range(groups)
        for a in range(n)
        for b in range(n)
    ]
    return lax.ppermute(values, EVERY, route)


def shifted(block, axis, distance):
    devices = range(lax.axis_size(axis))
    route = [(i - distance, i) for i in devices if i - distance in devices]
    return lax.ppermute(block, axis, route)


def copies(values, axis, count, groups=None):
    sent = jnp.broadcast_to(values[None], (count,) + values.shape)
    return lax.all_to_all(sent, axis, 0, 0, tiled=True, axis_index_groups=groups)


def total_of(blocks, axis, groups=None):
    got = lax.all_to_all(blocks, axis, 0, 0, tiled=True, axis_index_groups=groups)
    return jnp.sum(got.astype(F32), axis=0)


def contract_rows(left, right):
    return lax.dot_general(left, right, (((0,), (0,)), ((), ())), preferred_element_type=F32)


def to_feature_owners(blocks):
    return lax.all_to_all(blocks, "tensor", 0, 0, tiled=True)


def chip_order(own, other, core):
    pair = jnp.where(core == 0, jnp.stack([own, other], axis=1), jnp.stack([other, own], axis=1))
    return pair.reshape((own.shape[0] * 2,) + own.shape[1:])


def blocks_in_kernel(flipped, left, weight, out, total):
    step = pl.program_id(0)
    dims = (((1,), (1 if flipped else 0,)), ((), ()))
    part = lax.dot_general(left[0], weight[0], dims, preferred_element_type=F32)
    for k in range(1, left.shape[0]):
        part += lax.dot_general(left[k], weight[k], dims, preferred_element_type=F32)

    @pl.when(step == 0)
    def _():
        total[...] = part

    @pl.when(step > 0)
    def _():
        total[...] += part

    @pl.when(step == pl.num_programs(0) - 1)
    def _():
        out[...] = total[...].astype(out.dtype)


def product_in(left, weight, flipped, half, halves, each=2):
    n, rows, width = left.shape
    units = weight.shape[1 if flipped else 2] // halves
    if flipped:
        spec = pl.BlockSpec((each, units, width), lambda b: (b, half, 0))
    else:
        spec = pl.BlockSpec((each, width, units), lambda b: (b, 0, half))
    return pl.pallas_call(
        functools.partial(blocks_in_kernel, flipped),
        grid=(n // each,),
        in_specs=[pl.BlockSpec((each, rows, width), lambda b: (b, 0, 0)), spec],
        out_specs=pl.BlockSpec((rows, units), lambda b: (0, 0)),
        out_shape=jax.ShapeDtypeStruct((rows, units), BF16),
        scratch_shapes=[pltpu.VMEM((rows, units), F32)],
        compiler_params=pltpu.CompilerParams(vmem_limit_bytes=40 << 20),
        cost_estimate=pl.CostEstimate(
            flops=2 * n * rows * width * units,
            bytes_accessed=2 * n * width * (rows + units),
            transcendentals=0,
        ),
        name="product_in",
    )(left, weight)


def blocks_out_kernel(flipped, left, weight, *rest):
    out = rest[-1]
    rows = left.shape[0]
    dims = (((1,), (1 if flipped else 0,)), ((), ()))
    for k in range(weight.shape[0]):
        product = lax.dot_general(left[...], weight[k], dims, preferred_element_type=F32)
        out[k, :rows] = product.astype(out.dtype)
        if len(rest) == 2:
            out[k, rows:] = rest[0][...]


def product_out(left, weight, flipped, added=None, each=2):
    rows, units = left.shape
    n, first, second = weight.shape
    width = first if flipped else second
    extra = [] if added is None else [added]
    height = rows + sum(e.shape[0] for e in extra)
    return pl.pallas_call(
        functools.partial(blocks_out_kernel, flipped),
        grid=(n // each,),
        in_specs=[
            pl.BlockSpec((rows, units), lambda b: (0, 0)),
            pl.BlockSpec((each, first, second), lambda b: (b, 0, 0)),
        ]
        + [pl.BlockSpec(e.shape, lambda b: (0, 0)) for e in extra],
        out_specs=pl.BlockSpec((each, height, width), lambda b: (b, 0, 0)),
        out_shape=jax.ShapeDtypeStruct((n, height, width), BF16),
        compiler_params=pltpu.CompilerParams(vmem_limit_bytes=40 << 20),
        cost_estimate=pl.CostEstimate(
            flops=2 * n * rows * width * units,
            bytes_accessed=2 * n * width * (rows + units),
            transcendentals=0,
        ),
        name="product_out",
    )(left, weight, *extra)


def in_pieces(values, count, width):
    rows, rest = [], values
    for _ in range(3):
        rows.append(rest.astype(BF16))
        rest = rest - rows[-1].astype(F32)
    return jnp.pad(jnp.stack(rows), ((0, count - 3), (0, width - values.shape[0])))


def summed_in(left, weight, flipped, halves=2):
    own = [product_in(left, weight, flipped, k, halves) for k in range(halves)]
    other = [other_group(part) for part in own]
    return [p.astype(F32) + o.astype(F32) for p, o in zip(own, other)]


def after(values, *earlier):
    for other in earlier:
        first = other[(0,) * other.ndim].astype(F32)
        values = values + (0.0 * first).astype(values.dtype)
    return values


def body(
    context,
    low,
    mid,
    top,
    segments,
    output_weight,
    join_weight,
    inner_weight,
    outer_weight,
    norm_gain,
):
    n_dp = lax.axis_size("dp")
    n_tensor = lax.axis_size("tensor")
    chips = lax.axis_size(UNITS) // 2
    rows, width = context.shape
    rows_b, width_b = low.shape
    tokens = rows * n_dp
    core = lax.axis_index("tensor") % 2
    peers = chip_peers()
    place = lax.axis_index("tensor") * rows

    own_top = swap_axes(top)
    gain = norm_gain[:, None]
    following_top = shifted(own_top[: STEPS + 1], "tensor", -1)
    top_ext = jnp.concatenate([own_top, following_top], axis=0).astype(F32)
    seg_pad = jnp.concatenate([segments, jnp.full((STEPS + 1,), -1, jnp.int32)])
    seg_window = lax.dynamic_slice_in_dim(seg_pad, place, rows + STEPS + 1, 0)

    first_group = lax.axis_index("group") == 0
    hidden_all = []
    near = lax.all_gather(jnp.concatenate([low, mid], axis=1), "tensor", axis=0, tiled=True)
    half = near.reshape(n_tensor // 2, 2, rows_b, 2 * width_b)
    far_own = other_group(lax.dynamic_index_in_dim(half, core, 1, keepdims=False))
    far = chip_order(far_own, other_core(far_own), core).reshape(near.shape)
    for k in range(2):
        ours, theirs = (v[:, k * width_b : (k + 1) * width_b] for v in (near, far))
        hidden_all.append(
            jnp.where(
                first_group,
                jnp.concatenate([ours, theirs], axis=0),
                jnp.concatenate([theirs, ours], axis=0),
            )
        )
    gained = (inner_weight.astype(F32) * gain).astype(BF16)
    inner_all = lax.all_gather(gained, "tensor", axis=0, tiled=True)
    inner_all = inner_all.reshape(n_tensor, width, -1)
    outer_all = lax.all_gather(outer_weight, "tensor", axis=0, tiled=False)

    context_all = copies(context, "dp", n_dp).reshape(tokens, width)
    part = jnp.dot(context_all, output_weight, preferred_element_type=F32)
    part = after(part, own_top).astype(BF16)
    part = part.reshape(chips, 2, rows_b, width_b)
    kept = lax.dynamic_index_in_dim(part, core, 1, keepdims=False)
    given = lax.dynamic_index_in_dim(part, 1 - core, 1, keepdims=False)
    part = (kept.astype(F32) + other_core(given).astype(F32)).astype(BF16)
    high = after(mid.astype(F32), far_own, following_top) + total_of(part, UNITS, peers)
    high = high.astype(BF16)
    high_own = copies(high, UNITS, chips, peers)
    high_other = other_core(high_own)
    high_all = chip_order(high_own, high_other, core).reshape(tokens, width_b)
    hidden_all.append(high_all)

    joined = jnp.dot(hidden_all[0], join_weight[0], preferred_element_type=F32)
    joined = joined + jnp.dot(hidden_all[1], join_weight[1], preferred_element_type=F32)
    joined = joined + jnp.dot(hidden_all[2], join_weight[2], preferred_element_type=F32)
    joined = total_of(joined.astype(BF16).reshape(n_dp, rows, width), "dp")
    joined = joined.astype(BF16)
    state = swap_axes(joined)
    x_tokens = [lax.all_gather(joined, "dp", axis=0, tiled=True)]

    saved = []
    total = jnp.zeros((), F32)
    for step in range(STEPS):
        xfull = state.astype(F32)
        x_all = copies(state, "dp", n_dp)
        if step > 0:
            x_tokens.append(to_feature_owners(x_all).reshape(tokens, width))
        x_wide = x_all.astype(F32)
        sums = jnp.sum(x_wide * x_wide, axis=(0, 2))
        sums = sums + other_group(sums)
        scale = lax.rsqrt(sums / D + epsilon)[:, None]
        inner = scale * jnp.concatenate(summed_in(x_all, inner_all, False), axis=1)
        if step > 0:
            inner = after(inner, saved[0][3])
        active = jax.nn.silu(inner).astype(BF16)
        update = total_of(product_out(active, outer_all, False), "dp")
        following = (xfull + update).astype(BF16)
        valid = (seg_window[step + 1 : step + 1 + rows] == seg_window[:rows]).astype(F32)
        error = valid[:, None] * (following.astype(F32) - top_ext[step + 1 : step + 1 + rows])
        total = total + jnp.sum(error * error)
        active_all = lax.all_gather(active, "tensor", axis=0, tiled=True)
        saved.append((xfull, scale, inner, active_all, error))
        state = following
    scaled_all, sources = [], []
    rate = 1.0 / math.sqrt(tokens)
    grad = jnp.zeros((rows, width), F32)
    grad_inner = jnp.zeros(inner_weight.shape, F32)
    grad_outer = jnp.zeros(outer_weight.shape, F32)
    for step in reversed(range(STEPS)):
        xfull, scale, inner, active_all, error = saved[step]
        grad = grad + rate * error
        grad_half = grad.astype(BF16)
        grad_all = copies(grad_half, "dp", n_dp)
        grad_tokens = to_feature_owners(grad_all)
        back_act = jnp.concatenate(summed_in(grad_all, outer_all, True), axis=1)
        if step == 0:
            back_act = after(back_act, grad_tokens)
        if step < STEPS - 1:
            back_act = after(back_act, mean_error)
        else:
            back_act = after(back_act, *x_tokens)
        grad_tokens = grad_tokens.reshape(tokens, width)
        sigma = jax.nn.sigmoid(inner)
        grad_in = (back_act * sigma * (1.0 + inner * (1.0 - sigma))).astype(BF16)
        grad_in_wide = grad_in.astype(F32)
        moved = jnp.sum(grad_in_wide * inner, axis=1)
        moved = in_pieces(jnp.concatenate([moved, total[None]]), 16, width)
        back = total_of(product_out(grad_in, inner_all, True, moved), "dp")
        back_norm = back[:rows]
        moved = back[rows] + back[rows + 1] + back[rows + 2]
        if step == STEPS - 1:
            total_dp = jnp.broadcast_to(moved[rows], (128,))
        moved = moved[:rows, None]
        grad = grad + scale * back_norm - xfull * scale**2 * moved / D
        sources.append((active_all, grad_tokens))
        if step == 0:
            grad_outer = contract_rows(active_all, grad_tokens)
            grad = after(grad, grad_outer)
        scaled = (scale * grad_in_wide).astype(BF16)
        scaled_all.append(lax.all_gather(scaled, "tensor", axis=0, tiled=True))
        if step == STEPS - 1:
            for k in (1, 2, 4):
                total_dp = total_dp + lax.ppermute(
                    total_dp, "tensor", [(i, i ^ k) for i in range(n_tensor)]
                )
            mean_error = (total_dp + other_group(total_dp))[0] / (STEPS * tokens * D)
    swapped = after(swap_axes(grad.astype(BF16)), *[source[1] for source in sources])
    for units, features in sources[:-1]:
        grad_outer = grad_outer + contract_rows(units, features)
    for step, units in zip(reversed(range(STEPS)), scaled_all):
        grad_inner = grad_inner + gain * contract_rows(x_tokens[step], units)
    grad_tokens = copies(swapped, "dp", n_dp).reshape(tokens, width)
    grad_tokens = after(grad_tokens, grad_inner, grad_outer)
    grad_join = jnp.stack([contract_rows(source, grad_tokens) for source in hidden_all])
    return (mean_error, grad_join, grad_inner, grad_outer)


def solution(mesh):
    in_specs = (
        P("dp", ("group", "tensor")),
        P(("group", "tensor"), "dp"),
        P(("group", "tensor"), "dp"),
        P("dp", ("group", "tensor")),
        P(),
        P(("group", "tensor"), "dp"),
        P(None, "dp", ("group", "tensor")),
        P(("group", "tensor"), "dp"),
        P("dp", ("group", "tensor")),
        P(("group", "tensor")),
    )
    out_specs = (
        P(),
        P(None, "dp", ("group", "tensor")),
        P(("group", "tensor"), "dp"),
        P("dp", ("group", "tensor")),
    )
    return jax.shard_map(body, mesh=mesh, in_specs=in_specs, out_specs=out_specs, check_vma=False)
```

```python
import functools
import math

import jax
import jax.numpy as jnp
from jax import lax
from jax.experimental import pallas as pl
from jax.experimental.pallas import tpu as pltpu
from jax.sharding import PartitionSpec as P

D = 8192
STEPS = 2
epsilon = 1e-05

F32 = jnp.float32
BF16 = jnp.bfloat16
UNITS = ("group", "tensor")
EVERY = ("group", "dp", "tensor")


def chip_peers():
    n = lax.axis_size(UNITS)
    return [[chip * 2 + core for chip in range(n // 2)] for core in range(2)]


def other_core(values):
    n = lax.axis_size("tensor")
    return lax.ppermute(values, "tensor", [(i, i ^ 1) for i in range(n)])


def other_group(values):
    return lax.ppermute(values, "group", [(0, 1), (1, 0)])


def swap_axes(values):
    groups, n = lax.axis_size("group"), lax.axis_size("dp")
    route = [
        ((k * n + a) * n + b, (k * n + b) * n + a)
        for k in range(groups)
        for a in range(n)
        for b in range(n)
    ]
    return lax.ppermute(values, EVERY, route)


def shifted(block, axis, distance):
    devices = range(lax.axis_size(axis))
    route = [(i - distance, i) for i in devices if i - distance in devices]
    return lax.ppermute(block, axis, route)


def copies(values, axis, count, groups=None):
    sent = jnp.broadcast_to(values[None], (count,) + values.shape)
    return lax.all_to_all(sent, axis, 0, 0, tiled=True, axis_index_groups=groups)


def total_of(blocks, axis, groups=None):
    got = lax.all_to_all(blocks, axis, 0, 0, tiled=True, axis_index_groups=groups)
    return jnp.sum(got.astype(F32), axis=0)


def contract_rows(left, right):
    return lax.dot_general(left, right, (((0,), (0,)), ((), ())), preferred_element_type=F32)


def to_feature_owners(blocks):
    return lax.all_to_all(blocks, "tensor", 0, 0, tiled=True)


def chip_order(own, other, core):
    pair = jnp.where(core == 0, jnp.stack([own, other], axis=1), jnp.stack([other, own], axis=1))
    return pair.reshape((own.shape[0] * 2,) + own.shape[1:])


def blocks_in_kernel(flipped, left, weight, out, total):
    step = pl.program_id(0)
    dims = (((1,), (1 if flipped else 0,)), ((), ()))
    part = lax.dot_general(left[0], weight[0], dims, preferred_element_type=F32)
    for k in range(1, left.shape[0]):
        part += lax.dot_general(left[k], weight[k], dims, preferred_element_type=F32)

    @pl.when(step == 0)
    def _():
        total[...] = part

    @pl.when(step > 0)
    def _():
        total[...] += part

    @pl.when(step == pl.num_programs(0) - 1)
    def _():
        out[...] = total[...].astype(out.dtype)


def product_in(left, weight, flipped, half, halves, each=2):
    n, rows, width = left.shape
    units = weight.shape[1 if flipped else 2] // halves
    if flipped:
        spec = pl.BlockSpec((each, units, width), lambda b: (b, half, 0))
    else:
        spec = pl.BlockSpec((each, width, units), lambda b: (b, 0, half))
    return pl.pallas_call(
        functools.partial(blocks_in_kernel, flipped),
        grid=(n // each,),
        in_specs=[pl.BlockSpec((each, rows, width), lambda b: (b, 0, 0)), spec],
        out_specs=pl.BlockSpec((rows, units), lambda b: (0, 0)),
        out_shape=jax.ShapeDtypeStruct((rows, units), BF16),
        scratch_shapes=[pltpu.VMEM((rows, units), F32)],
        compiler_params=pltpu.CompilerParams(vmem_limit_bytes=40 << 20),
        cost_estimate=pl.CostEstimate(
            flops=2 * n * rows * width * units,
            bytes_accessed=2 * n * width * (rows + units),
            transcendentals=0,
        ),
        name="product_in",
    )(left, weight)


def blocks_out_kernel(flipped, left, weight, *rest):
    out = rest[-1]
    rows = left.shape[0]
    dims = (((1,), (1 if flipped else 0,)), ((), ()))
    for k in range(weight.shape[0]):
        product = lax.dot_general(left[...], weight[k], dims, preferred_element_type=F32)
        out[k, :rows] = product.astype(out.dtype)
        if len(rest) == 2:
            out[k, rows:] = rest[0][...]


def product_out(left, weight, flipped, added=None, each=2):
    rows, units = left.shape
    n, first, second = weight.shape
    width = first if flipped else second
    extra = [] if added is None else [added]
    height = rows + sum(e.shape[0] for e in extra)
    return pl.pallas_call(
        functools.partial(blocks_out_kernel, flipped),
        grid=(n // each,),
        in_specs=[
            pl.BlockSpec((rows, units), lambda b: (0, 0)),
            pl.BlockSpec((each, first, second), lambda b: (b, 0, 0)),
        ]
        + [pl.BlockSpec(e.shape, lambda b: (0, 0)) for e in extra],
        out_specs=pl.BlockSpec((each, height, width), lambda b: (b, 0, 0)),
        out_shape=jax.ShapeDtypeStruct((n, height, width), BF16),
        compiler_params=pltpu.CompilerParams(vmem_limit_bytes=40 << 20),
        cost_estimate=pl.CostEstimate(
            flops=2 * n * rows * width * units,
            bytes_accessed=2 * n * width * (rows + units),
            transcendentals=0,
        ),
        name="product_out",
    )(left, weight, *extra)


def in_pieces(values, count, width):
    rows, rest = [], values
    for _ in range(3):
        rows.append(rest.astype(BF16))
        rest = rest - rows[-1].astype(F32)
    return jnp.pad(jnp.stack(rows), ((0, count - 3), (0, width - values.shape[0])))


def summed_in(left, weight, flipped, halves=2):
    own = [product_in(left, weight, flipped, k, halves) for k in range(halves)]
    other = [other_group(part) for part in own]
    return [p.astype(F32) + o.astype(F32) for p, o in zip(own, other)]


def after(values, *earlier):
    for other in earlier:
        first = other[(0,) * other.ndim].astype(F32)
        values = values + (0.0 * first).astype(values.dtype)
    return values


def body(
    context,
    low,
    mid,
    top,
    segments,
    output_weight,
    join_weight,
    inner_weight,
    outer_weight,
    norm_gain,
):
    n_dp = lax.axis_size("dp")
    n_tensor = lax.axis_size("tensor")
    chips = lax.axis_size(UNITS) // 2
    rows, width = context.shape
    rows_b, width_b = low.shape
    tokens = rows * n_dp
    core = lax.axis_index("tensor") % 2
    peers = chip_peers()
    place = lax.axis_index("tensor") * rows

    own_top = swap_axes(top)
    gain = norm_gain[:, None]
    following_top = shifted(own_top[: STEPS + 1], "tensor", -1)
    top_ext = jnp.concatenate([own_top, following_top], axis=0).astype(F32)
    seg_pad = jnp.concatenate([segments, jnp.full((STEPS + 1,), -1, jnp.int32)])
    seg_window = lax.dynamic_slice_in_dim(seg_pad, place, rows + STEPS + 1, 0)

    first_group = lax.axis_index("group") == 0
    hidden_all = []
    near = lax.all_gather(jnp.concatenate([low, mid], axis=1), "tensor", axis=0, tiled=True)
    half = near.reshape(n_tensor // 2, 2, rows_b, 2 * width_b)
    far_own = other_group(lax.dynamic_index_in_dim(half, core, 1, keepdims=False))
    far = chip_order(far_own, other_core(far_own), core).reshape(near.shape)
    for k in range(2):
        ours, theirs = (v[:, k * width_b : (k + 1) * width_b] for v in (near, far))
        hidden_all.append(
            jnp.where(
                first_group,
                jnp.concatenate([ours, theirs], axis=0),
                jnp.concatenate([theirs, ours], axis=0),
            )
        )
    gained = (inner_weight.astype(F32) * gain).astype(BF16)
    inner_all = lax.all_gather(gained, "tensor", axis=0, tiled=True)
    inner_all = inner_all.reshape(n_tensor, width, -1)
    outer_all = lax.all_gather(outer_weight, "tensor", axis=0, tiled=False)

    context_all = copies(context, "dp", n_dp).reshape(tokens, width)
    part = jnp.dot(context_all, output_weight, preferred_element_type=F32)
    part = after(part, own_top).astype(BF16)
    part = part.reshape(chips, 2, rows_b, width_b)
    kept = lax.dynamic_index_in_dim(part, core, 1, keepdims=False)
    given = lax.dynamic_index_in_dim(part, 1 - core, 1, keepdims=False)
    part = (kept.astype(F32) + other_core(given).astype(F32)).astype(BF16)
    high = after(mid.astype(F32), far_own, following_top) + total_of(part, UNITS, peers)
    high = high.astype(BF16)
    high_own = copies(high, UNITS, chips, peers)
    high_other = other_core(high_own)
    high_all = chip_order(high_own, high_other, core).reshape(tokens, width_b)
    hidden_all.append(high_all)

    joined = jnp.dot(hidden_all[0], join_weight[0], preferred_element_type=F32)
    joined = joined + jnp.dot(hidden_all[1], join_weight[1], preferred_element_type=F32)
    joined = joined + jnp.dot(hidden_all[2], join_weight[2], preferred_element_type=F32)
    joined = total_of(joined.astype(BF16).reshape(n_dp, rows, width), "dp")
    joined = joined.astype(BF16)
    state = swap_axes(joined)
    x_tokens = [lax.all_gather(joined, "dp", axis=0, tiled=True)]

    saved = []
    total = jnp.zeros((), F32)
    for step in range(STEPS):
        xfull = state.astype(F32)
        x_all = copies(state, "dp", n_dp)
        if step > 0:
            x_tokens.append(to_feature_owners(x_all).reshape(tokens, width))
        x_wide = x_all.astype(F32)
        sums = jnp.sum(x_wide * x_wide, axis=(0, 2))
        sums = sums + other_group(sums)
        scale = lax.rsqrt(sums / D + epsilon)[:, None]
        inner = scale * jnp.concatenate(summed_in(x_all, inner_all, False), axis=1)
        if step > 0:
            inner = after(inner, saved[0][3])
        active = jax.nn.silu(inner).astype(BF16)
        update = total_of(product_out(active, outer_all, False), "dp")
        following = (xfull + update).astype(BF16)
        valid = (seg_window[step + 1 : step + 1 + rows] == seg_window[:rows]).astype(F32)
        error = valid[:, None] * (following.astype(F32) - top_ext[step + 1 : step + 1 + rows])
        total = total + jnp.sum(error * error)
        active_all = lax.all_gather(active, "tensor", axis=0, tiled=True)
        saved.append((xfull, scale, inner, active_all, error))
        state = following
    scaled_all = []
    rate = 1.0 / math.sqrt(tokens)
    grad = jnp.zeros((rows, width), F32)
    grad_inner = jnp.zeros(inner_weight.shape, F32)
    grad_outer = jnp.zeros(outer_weight.shape, F32)
    for step in reversed(range(STEPS)):
        xfull, scale, inner, active_all, error = saved[step]
        grad = grad + rate * error
        grad_half = grad.astype(BF16)
        grad_all = copies(grad_half, "dp", n_dp)
        grad_tokens = to_feature_owners(grad_all)
        back_act = jnp.concatenate(summed_in(grad_all, outer_all, True), axis=1)
        back_act = after(back_act, grad_tokens)
        if step < STEPS - 1:
            back_act = after(back_act, mean_error)
        else:
            back_act = after(back_act, *x_tokens)
        grad_tokens = grad_tokens.reshape(tokens, width)
        sigma = jax.nn.sigmoid(inner)
        grad_in = (back_act * sigma * (1.0 + inner * (1.0 - sigma))).astype(BF16)
        grad_in_wide = grad_in.astype(F32)
        moved = jnp.sum(grad_in_wide * inner, axis=1)
        moved = in_pieces(jnp.concatenate([moved, total[None]]), 16, width)
        back = total_of(product_out(grad_in, inner_all, True, moved), "dp")
        back_norm = back[:rows]
        moved = back[rows] + back[rows + 1] + back[rows + 2]
        if step == STEPS - 1:
            total_dp = jnp.broadcast_to(moved[rows], (128,))
        moved = moved[:rows, None]
        grad = grad + scale * back_norm - xfull * scale**2 * moved / D
        grad_outer = grad_outer + contract_rows(active_all, grad_tokens)
        if step == 0:
            grad = after(grad, grad_outer)
        scaled = (scale * grad_in_wide).astype(BF16)
        scaled_all.append(lax.all_gather(scaled, "tensor", axis=0, tiled=True))
        if step == STEPS - 1:
            for k in (1, 2, 4):
                total_dp = total_dp + lax.ppermute(
                    total_dp, "tensor", [(i, i ^ k) for i in range(n_tensor)]
                )
            mean_error = (total_dp + other_group(total_dp))[0] / (STEPS * tokens * D)
    swapped = after(swap_axes(grad.astype(BF16)), *x_tokens)
    for step, units in zip(reversed(range(STEPS)), scaled_all):
        grad_inner = grad_inner + gain * contract_rows(x_tokens[step], units)
    grad_tokens = copies(swapped, "dp", n_dp).reshape(tokens, width)
    grad_tokens = after(grad_tokens, grad_inner)
    grad_join = jnp.stack([contract_rows(source, grad_tokens) for source in hidden_all])
    return (mean_error, grad_join, grad_inner, grad_outer)


def solution(mesh):
    in_specs = (
        P("dp", ("group", "tensor")),
        P(("group", "tensor"), "dp"),
        P(("group", "tensor"), "dp"),
        P("dp", ("group", "tensor")),
        P(),
        P(("group", "tensor"), "dp"),
        P(None, "dp", ("group", "tensor")),
        P(("group", "tensor"), "dp"),
        P("dp", ("group", "tensor")),
        P(("group", "tensor")),
    )
    out_specs = (
        P(),
        P(None, "dp", ("group", "tensor")),
        P(("group", "tensor"), "dp"),
        P("dp", ("group", "tensor")),
    )
    return jax.shard_map(body, mesh=mesh, in_specs=in_specs, out_specs=out_specs, check_vma=False)
```
